32 devices in a mesh: grp: 4 (over x, core), shard: 8 (over z, y).
Axes of the slice: x: 2, y: 2, z: 4, core: 2. Of those that a mesh axis runs over, the one named last changes fastest.
Arguments:
- inputs: bfloat16 [2, 1024, 4096], P(None, None, 'grp'), may hold values from -6 to 6
- up_cotangent: bfloat16 [2, 1024, 14336], P(None, None, 'shard'), may hold values from -0.1875 to 0.1875
- signs: int32 [4096, 16384], P('grp', 'shard'), may hold values from -1 to 1, as said below
- kept_row: int32 [8192], replicated, may hold values from 0 to 4095
- kept_col: int32 [8192], replicated, may hold values from 0 to 16383
Outputs:
- features: float32 [2, 8192], P(None, ('grp', 'shard'))
The draws below stay inside these ranges and needn't reach their ends.
Inputs may be any that keep to these rules, and one draw needn't show every extreme that they name: `signs`: every entry is -1 or +1.
All inputs are finite; a program needn't handle non-finite values.
Results may differ from the reference program's by a relative error of at most 0.0003.
Values sent between devices are 32-bit elements; how exact they have to be, the bound alone decides.
No kernel may reach another device: no remote copies, remote signals or barrier semaphores. Data moves between devices by JAX's collectives and lax.ppermute only.
A program may use at most 320 MiB of HBM per device.

```python
import math
import jax
import jax.numpy as jnp

D = 4096
FF = 14336
FPAD = 16384
KEPT = 8192
S = 1024
EXAMPLES = 2
N_SHARD = 8


def draw_signs(key, part):
    key = jax.random.fold_in(key, 11)
    coins = jax.random.randint(key, (D, FPAD), 0, 2, dtype=jnp.int32)
    return 2 * coins - 1


def place_ends(entries, rng, least, largest):
    spot = [jax.random.randint(jax.random.fold_in(rng, axis), (), 0, length) for axis, length in enumerate(entries.shape)]
    main_axis = entries.shape.index(max(entries.shape))
    neighbour = spot[:main_axis] + [(spot[main_axis] + 1) % entries.shape[main_axis]] + spot[main_axis + 1:]
    return entries.at[tuple(spot)].set(least).at[tuple(neighbour)].set(largest)


def level_of(rng, dims, pieces, least, top_value):
    factor_of = 1.0
    for axis_at, shards_of in pieces:
        draws = jax.random.uniform(jax.random.fold_in(jax.random.fold_in(rng, 6), axis_at), (shards_of,), jnp.float32, least / len(pieces), top_value / len(pieces))
        factor_of = factor_of * jnp.repeat(jnp.exp(draws), dims[axis_at] // shards_of).reshape((-1,) + (1,) * (len(dims) - 1 - axis_at))
    return factor_of


def gaussian(own_key, extent, deviation, most, pieces=(), held_as=jnp.bfloat16):
    array = deviation * jax.random.normal(own_key, extent, jnp.float32)
    if pieces:
        array = array * level_of(own_key, extent, pieces, -0.22, 0.18)
    return jnp.clip(array, -most, most).astype(held_as)


def setup_inputs(seed: int = 0) -> dict:
    key_of = jax.random.split(jax.random.key(seed), 6)
    inputs = gaussian(key_of[0], (EXAMPLES, S, D), 1.0, 6.0, ((2, 4),))
    up_cotangent = gaussian(key_of[1], (EXAMPLES, S, FF), (S ** -0.5), 0.1875, ((2, 8),))
    signs = draw_signs(jax.random.fold_in(key_of[5], 71), 0)
    kept_row = place_ends(jax.random.randint(key_of[3], (KEPT,), 0, D), jax.random.fold_in(key_of[3], 1), 0, D - 1).astype(jnp.int32)
    kept_col = place_ends(jax.random.randint(key_of[4], (KEPT,), 0, FPAD), jax.random.fold_in(key_of[4], 1), 0, FPAD - 1).astype(jnp.int32)
    return {"inputs": inputs, "up_cotangent": up_cotangent, "signs": signs, "kept_row": kept_row, "kept_col": kept_col}


def walsh_transform(flat_values):
    length = flat_values.shape[0]
    half_width = 1
    while half_width < length:
        paired = flat_values.reshape(-1, 2, half_width)
        flat_values = jnp.stack([paired[:, 0] + paired[:, 1], paired[:, 0] - paired[:, 1]], axis=1).reshape(-1)
        half_width = half_width * 2
    return flat_values

def reference(inputs, up_cotangent, signs, kept_row, kept_col):
    results = []
    for example in range(EXAMPLES):
        gradient = jnp.dot(inputs[example].T, up_cotangent[example], preferred_element_type=jnp.float32)
        gradient = gradient.reshape(D, N_SHARD, FF // N_SHARD)
        gradient = jnp.pad(gradient, ((0, 0), (0, 0), (0, FPAD // N_SHARD - FF // N_SHARD)))
        placed = gradient.reshape(D, FPAD)
        signed = placed * signs.astype(jnp.float32)
        transformed = walsh_transform(signed.reshape(-1)).reshape(D, FPAD)
        results.append(transformed[kept_row, kept_col] / math.sqrt(D * FPAD))
    return jnp.stack(results)
```

```python
import math

import jax
import jax.numpy as jnp
import numpy as np
from jax import lax
from jax.experimental import pallas as pl
from jax.experimental.pallas import tpu as pltpu
from jax.sharding import PartitionSpec as P

D = 4096
FPAD = 16384
LANES = 128
TILE = 256


def hadamard(length):
    table = np.ones((1, 1), np.float32)
    while table.shape[0] < length:
        table = np.block([[table, table], [table, -table]])
    return table


def interleaved_table():
    h = hadamard(LANES)
    table = np.zeros((LANES, 2, 2, LANES), np.float32)
    table[:, 0, 0, :] = h
    table[:, 1, 1, :] = h
    return table.reshape(2 * LANES, 2 * LANES)


def butterflies(blocks):
    blocks = list(blocks)
    width = 1
    while width < len(blocks):
        for low in range(len(blocks)):
            if low & width:
                continue
            a, b = blocks[low], blocks[low | width]
            if b is None:
                blocks[low | width] = a
            else:
                blocks[low], blocks[low | width] = a + b, a - b
        width *= 2
    return blocks


def split(values):
    high = values.astype(jnp.bfloat16)
    low = (values - high.astype(jnp.float32)).astype(jnp.bfloat16)
    return high, low


def parity_sign(bits):
    for shift in (16, 8, 4, 2, 1):
        bits = jnp.bitwise_xor(bits, jnp.right_shift(bits, shift))
    return (1 - 2 * jnp.bitwise_and(bits, 1)).astype(jnp.float32)


def sketch_kernel(row_count, column_count, tiles,
                  position_ref, x_ref, u_ref, signs_ref, kept_row_ref, kept_col_ref, row_table_ref, lane_table_ref,
                  out_ref,
                  xt, signed, table, spot_vmem, spot_smem, stage_a, stage_b, spot_sem):
    step = pl.program_id(0)
    row_blocks = row_count // LANES
    column_blocks = column_count // LANES
    pairs = column_blocks // 2
    chunks = kept_row_ref.shape[0]
    f32 = jnp.float32

    def spot_copy():
        return pltpu.make_async_copy(spot_vmem, spot_smem, spot_sem)

    @pl.when(step == 0)
    def _():
        row = jnp.bitwise_and(kept_row_ref[...], row_count - 1)
        col = jnp.bitwise_and(kept_col_ref[...], column_count - 1)
        block = (row // LANES) * column_blocks + col // LANES
        spot_vmem[...] = (block * LANES + jnp.bitwise_and(row, LANES - 1)) * 2
        spot_copy().start()
        for e in range(2):
            for block in range(row_blocks):
                cut = slice(block * LANES, (block + 1) * LANES)
                xt[e, cut, :] = x_ref[e, :, cut].T

    for block in range(row_blocks):
        cut = slice(block * LANES, (block + 1) * LANES)
        block_signs = signs_ref[cut, :].astype(f32)
        for e in range(2):
            product = jnp.dot(xt[e, cut, :], u_ref[e], preferred_element_type=f32)
            signed[block, e * LANES:(e + 1) * LANES, :] = product * block_signs

    group = 16
    for start in range(0, 2 * LANES, group):
        rows = slice(start, start + group)
        blocks = butterflies([signed[block, rows, :] for block in range(row_blocks)])
        for block in range(row_blocks):
            signed[block, rows, :] = blocks[block]

    for block in range(row_blocks):
        high, low = split(signed[block])
        whole = jnp.dot(row_table_ref[...], high, preferred_element_type=f32)
        whole += jnp.dot(row_table_ref[...], low, preferred_element_type=f32)
        left, right = whole[:, :LANES], whole[:, LANES:]
        base = pl.multiple_of((block * column_blocks + 2 * step) * TILE, TILE)
        table[pl.ds(base, TILE), :] = left + right
        table[pl.ds(base + TILE, TILE), :] = left - right

    @pl.when(step == tiles - 1)
    def _():
        if pairs > 1:
            part = 32

            def columns(at, carry):
                block = at // (TILE // part)
                row = (at % (TILE // part)) * part
                base = pl.multiple_of(block * (column_blocks * TILE) + row, 8)
                for half in range(2):
                    for extra in range(0, part, 8):
                        def place(pair):
                            return pl.ds(base + (2 * pair + half) * TILE + extra, 8)

                        blocks = butterflies(
                            [table[place(pair), :] if pair < tiles else None for pair in range(pairs)])
                        for pair in range(pairs):
                            table[place(pair), :] = blocks[pair]
                return carry

            lax.fori_loop(0, row_blocks * (TILE // part), columns, 0)
        spot_copy().wait()

        def gather(chunk, stage):
            for u in range(LANES):
                at = pl.multiple_of(spot_smem[chunk, u], 2)
                stage[2 * u:2 * u + 2, :] = table[pl.ds(at, 2), :]

        lane_table = lane_table_ref[...]
        scale = 1.0 / math.sqrt(D * FPAD)

        def finish(chunk, stage):
            rows = jnp.concatenate([stage[pl.ds(0, LANES, stride=2), :], stage[pl.ds(1, LANES, stride=2), :]], axis=0)
            high, low = split(rows)
            both = jnp.concatenate([high, low], axis=1)
            whole = lax.dot_general(lane_table, both, (((1,), (1,)), ((), ())), preferred_element_type=f32)
            kept_row = kept_row_ref[pl.ds(chunk, 1), :]
            kept_col = kept_col_ref[pl.ds(chunk, 1), :]
            lane = jnp.bitwise_and(kept_col, LANES - 1)
            sign = scale * parity_sign(jnp.bitwise_xor(
                jnp.bitwise_and(kept_row // row_count, position_ref[0]),
                jnp.bitwise_and(kept_col // column_count, position_ref[1])))
            mask = lax.broadcasted_iota(jnp.int32, (LANES, LANES), 0) == lane
            for e in range(2):
                picked = jnp.where(mask, whole[:, e * LANES:(e + 1) * LANES], 0.0)
                out_ref[e, pl.ds(chunk, 1), :] = jnp.sum(picked, axis=0, keepdims=True) * sign

        gather(0, stage_a)

        def two_chunks(at, carry):
            gather(2 * at + 1, stage_b)
            finish(2 * at, stage_a)
            gather(jnp.minimum(2 * at + 2, chunks - 1), stage_a)
            finish(2 * at + 1, stage_b)
            return carry

        lax.fori_loop(0, chunks // 2, two_chunks, 0)


def partial_features(position, inputs, up_cotangent, signs, kept_row, kept_col):
    examples, depth, row_count = inputs.shape
    column_count = signs.shape[1]
    if up_cotangent.shape[2] % TILE:
        extra = -up_cotangent.shape[2] % TILE
        up_cotangent = jnp.pad(up_cotangent, ((0, 0), (0, 0), (0, extra)))
    tiles = up_cotangent.shape[2] // TILE
    chunks = kept_row.shape[0] // LANES
    row_table = jnp.asarray(interleaved_table(), jnp.bfloat16)
    lane_table = jnp.asarray(np.concatenate([hadamard(LANES)] * 2, axis=1), jnp.bfloat16)
    whole = pl.BlockSpec(memory_space=pltpu.VMEM)
    return pl.pallas_call(
        lambda *refs: sketch_kernel(row_count, column_count, tiles, *refs),
        grid=(tiles,),
        in_specs=[
            pl.BlockSpec(memory_space=pltpu.SMEM),
            whole,
            pl.BlockSpec((examples, depth, TILE), lambda j: (0, 0, j)),
            pl.BlockSpec((row_count, TILE), lambda j: (0, j)),
            whole,
            whole,
            whole,
            whole,
        ],
        out_specs=pl.BlockSpec((examples, chunks, LANES), lambda j: (0, 0, 0)),
        out_shape=jax.ShapeDtypeStruct((examples, chunks, LANES), jnp.float32),
        scratch_shapes=[
            pltpu.VMEM((examples, row_count, depth), jnp.bfloat16),
            pltpu.VMEM((row_count // LANES, 2 * LANES, TILE), jnp.float32),
            pltpu.VMEM((row_count * 2 * (column_count // LANES), LANES), jnp.float32),
            pltpu.VMEM((chunks, LANES), jnp.int32),
            pltpu.SMEM((chunks, LANES), jnp.int32),
            pltpu.VMEM((2 * LANES, LANES), jnp.float32),
            pltpu.VMEM((2 * LANES, LANES), jnp.float32),
            pltpu.SemaphoreType.DMA,
        ],
        compiler_params=pltpu.CompilerParams(vmem_limit_bytes=60 * 1024 * 1024),
    )(position, inputs, up_cotangent, signs, kept_row.reshape(chunks, LANES), kept_col.reshape(chunks, LANES),
      row_table, lane_table)


def local(inputs, up_cotangent, signs, kept_row, kept_col):
    examples = inputs.shape[0]
    position = jnp.stack([lax.axis_index("grp"), lax.axis_index("shard")]).astype(jnp.int32)
    partial = partial_features(position, inputs, up_cotangent, signs, kept_row, kept_col)
    devices = lax.axis_size("grp") * lax.axis_size("shard")
    own = kept_row.shape[0] // devices
    shares = partial.reshape(examples, devices, own).transpose(1, 0, 2)
    shares = lax.all_to_all(shares, ("grp", "shard"), 0, 0, tiled=True)
    return jnp.sum(shares, axis=0)


def solution(mesh):
    placed = (P(None, None, "grp"), P(None, None, "shard"), P("grp", "shard"), P(), P())
    return jax.shard_map(
        local, mesh=mesh, in_specs=placed, out_specs=P(None, ("grp", "shard")), check_vma=False
    )
```

```python
import math

import jax
import jax.numpy as jnp
import numpy as np
from jax import lax
from jax.experimental import pallas as pl
from jax.experimental.pallas import tpu as pltpu
from jax.sharding import PartitionSpec as P

D = 4096
FPAD = 16384
LANES = 128
TILE = 256
BLOCK_STRIDE = TILE + 8
X_PIECES = 2
GROUP = 4
SLOTS = 4


def hadamard(length):
    table = np.ones((1, 1), np.float32)
    while table.shape[0] < length:
        table = np.block([[table, table], [table, -table]])
    return table


def interleaved_table():
    h = hadamard(LANES)
    table = np.zeros((LANES, 2, 2, LANES), np.float32)
    table[:, 0, 0, :] = h
    table[:, 1, 1, :] = h
    return table.reshape(2 * LANES, 2 * LANES)


def butterflies(blocks):
    blocks = list(blocks)
    width = 1
    while width < len(blocks):
        for low in range(len(blocks)):
            if low & width:
                continue
            a, b = blocks[low], blocks[low | width]
            if b is None:
                blocks[low | width] = a
            else:
                blocks[low], blocks[low | width] = a + b, a - b
        width *= 2
    return blocks


def split(values):
    high = values.astype(jnp.bfloat16)
    low = (values - high.astype(jnp.float32)).astype(jnp.bfloat16)
    return high, low


def parity_sign(bits):
    for shift in (16, 8, 4, 2, 1):
        bits = jnp.bitwise_xor(bits, jnp.right_shift(bits, shift))
    return (1 - 2 * jnp.bitwise_and(bits, 1)).astype(jnp.float32)


def sketch_kernel(row_count, column_count, tiles,
                  x_ref, u_ref, signs_ref, kept_row_ref, kept_col_ref, row_table_ref, lane_table_ref,
                  out_ref,
                  x, xt, u, signs, kept_row, kept_col, row_table, lane_table,
                  product, halves, table, factor, spot_vmem, spot_smem, stages,
                  x_sem, u_sem, signs_sem, small_sem, spot_sem):
    row_blocks = row_count // LANES
    column_blocks = column_count // LANES
    pairs = column_blocks // 2
    chunks = kept_row.shape[0]
    groups = chunks // GROUP
    group_at, shard_at = lax.axis_index("grp"), lax.axis_index("shard")
    f32 = jnp.float32

    def x_copy(e, piece):
        rows = pl.ds(piece * (x.shape[1] // X_PIECES), x.shape[1] // X_PIECES)
        return pltpu.make_async_copy(x_ref.at[e, rows], x.at[e, rows], x_sem.at[e, piece])

    def columns_of(tile):
        return pl.ds(pl.multiple_of(tile * TILE, TILE), TILE)

    def u_copy(tile):
        return pltpu.make_async_copy(u_ref.at[:, :, columns_of(tile)], u.at[tile], u_sem.at[tile])

    def signs_copy(tile):
        return pltpu.make_async_copy(signs_ref.at[:, columns_of(tile)], signs.at[tile], signs_sem.at[tile])

    def spot_copy(at, slot):
        return pltpu.make_async_copy(spot_vmem.at[at], spot_smem[slot], spot_sem.at[slot])

    small = [pltpu.make_async_copy(source, target, small_sem.at[at]) for at, (source, target) in enumerate(
        [(kept_row_ref, kept_row), (kept_col_ref, kept_col), (row_table_ref, row_table), (lane_table_ref, lane_table)])]

    def ahead(tile):
        u_copy(tile).start()
        signs_copy(tile).start()

    for e in range(2):
        for piece in range(X_PIECES):
            x_copy(e, piece).start()
        if e == 0:
            ahead(0)
    for copy in small:
        copy.start()

    def place(block, column_block):
        return (block * column_blocks + column_block) * BLOCK_STRIDE

    def turn(e):
        for piece in range(X_PIECES):
            x_copy(e, piece).wait()
        for block in range(row_blocks):
            cut = slice(block * LANES, (block + 1) * LANES)
            xt[e, cut, :] = x[e, :, cut].T

    def spread(e, tile, values):
        for start in range(0, LANES, 16):
            blocks = []
            for block in range(row_blocks):
                rows = slice(block * LANES + start, block * LANES + start + 16)
                blocks.append(values[rows, :] * signs[tile, rows, :].astype(f32))
            rows = slice(e * LANES + start, e * LANES + start + 16)
            for block, mixed in enumerate(butterflies(blocks)):
                halves[block, 0, rows, :], halves[block, 1, rows, :] = split(mixed)

    def gradient(e, tile):
        return jnp.dot(xt[e], u[tile, e], preferred_element_type=f32)

    def rows_to_table(tile):
        for block in range(row_blocks):
            whole = jnp.dot(row_table[...], halves[block, 0], preferred_element_type=f32)
            whole += jnp.dot(row_table[...], halves[block, 1], preferred_element_type=f32)
            left, right = whole[:, :LANES], whole[:, LANES:]
            table[pl.ds(pl.multiple_of(place(block, 2 * tile), 8), TILE), :] = left + right
            table[pl.ds(pl.multiple_of(place(block, 2 * tile + 1), 8), TILE), :] = left - right

    turn(0)
    u_copy(0).wait()
    first = gradient(0, 0)
    signs_copy(0).wait()
    for copy in small:
        copy.wait()
    for tile in range(1, min(3, tiles)):
        ahead(tile)
    spread(0, 0, first)
    turn(1)
    product[...] = gradient(1, 0)

    row = jnp.bitwise_and(kept_row[...], row_count - 1)
    col = jnp.bitwise_and(kept_col[...], column_count - 1)
    spots = place(row // LANES, col // LANES) + jnp.bitwise_and(row, LANES - 1) * 2
    for at in range(groups):
        spot_vmem[at] = spots[at * GROUP:(at + 1) * GROUP]
    for at in range(SLOTS):
        spot_copy(at, at).start()
    factor[...] = (1.0 / math.sqrt(D * FPAD)) * parity_sign(jnp.bitwise_xor(
        jnp.bitwise_and(kept_row[...] // row_count, group_at),
        jnp.bitwise_and(kept_col[...] // column_count, shard_at)))

    def later_tile(tile, carry):
        @pl.when(tile + 2 < tiles)
        def _():
            ahead(tile + 2)

        u_copy(tile).wait()
        signs_copy(tile).wait()
        first = gradient(0, tile)
        spread(1, tile - 1, product)
        rows_to_table(tile - 1)
        second = gradient(1, tile)
        spread(0, tile, first)
        product[...] = second
        return carry

    lax.fori_loop(1, tiles, later_tile, 0)
    spread(1, tiles - 1, product)
    rows_to_table(tiles - 1)

    if pairs > 1:
        part = 32

        def columns(at, carry):
            block = at // (TILE // part)
            row = (at % (TILE // part)) * part
            base = pl.multiple_of(place(block, 0) + row, 8)
            for half in range(2):
                for extra in range(0, part, 8):
                    def rows_of(pair):
                        return pl.ds(base + (2 * pair + half) * BLOCK_STRIDE + extra, 8)

                    blocks = butterflies(
                        [table[rows_of(pair), :] if pair < tiles else None for pair in range(pairs)])
                    for pair in range(pairs):
                        table[rows_of(pair), :] = blocks[pair]
            return carry

        lax.fori_loop(0, row_blocks * (TILE // part), columns, 0)

    def gather(slot, stage):
        for part in range(GROUP):
            for u_at in range(LANES):
                at = pl.multiple_of(spot_smem[slot][part, u_at], 2)
                stage[part, 2 * u_at:2 * u_at + 2, :] = table[pl.ds(at, 2), :]

    def finish(at, stage):
        for part in range(GROUP):
            finish_chunk(at * GROUP + part, stage.at[part])

    def finish_chunk(chunk, stage):
        rows = jnp.concatenate([stage[pl.ds(0, LANES, stride=2), :], stage[pl.ds(1, LANES, stride=2), :]], axis=0)
        high, low = split(rows)
        both = jnp.concatenate([high, low], axis=1)
        whole = lax.dot_general(lane_table[...], both, (((1,), (1,)), ((), ())), preferred_element_type=f32)
        lane = jnp.bitwise_and(kept_col[pl.ds(chunk, 1), :], LANES - 1)
        sign = factor[pl.ds(chunk, 1), :]
        mask = lax.broadcasted_iota(jnp.int32, (LANES, LANES), 0) == lane
        for e in range(2):
            picked = jnp.where(mask, whole[:, e * LANES:(e + 1) * LANES], 0.0)
            out_ref[chunk, pl.ds(e, 1), :] = jnp.sum(picked, axis=0, keepdims=True) * sign

    spot_copy(0, 0).wait()
    gather(0, stages[0])
    spot_copy(min(SLOTS, groups - 1), 0).start()

    def slots_round(turn_at, carry):
        for step in range(1, SLOTS + 1):
            at = turn_at * SLOTS + step
            slot = step % SLOTS
            spot_copy(jnp.minimum(at, groups - 1), slot).wait()
            gather(slot, stages[step % 2])
            finish(at - 1, stages[(step - 1) % 2])
            spot_copy(jnp.minimum(at + SLOTS, groups - 1), slot).start()
        return carry

    lax.fori_loop(0, groups // SLOTS, slots_round, 0)
    for slot in range(SLOTS):
        spot_copy(groups - 1, slot).wait()


def partial_features(inputs, up_cotangent, signs, kept_row, kept_col):
    examples, depth, row_count = inputs.shape
    column_count = signs.shape[1]
    if up_cotangent.shape[2] % TILE:
        extra = -up_cotangent.shape[2] % TILE
        up_cotangent = jnp.pad(up_cotangent, ((0, 0), (0, 0), (0, extra)))
    tiles = up_cotangent.shape[2] // TILE
    chunks = kept_row.shape[0] // LANES
    row_table = jnp.asarray(interleaved_table(), jnp.bfloat16)
    lane_table = jnp.asarray(np.concatenate([hadamard(LANES)] * 2, axis=1), jnp.bfloat16)
    there = pl.BlockSpec(memory_space=pl.ANY)
    row_blocks = row_count // LANES
    return pl.pallas_call(
        lambda *refs: sketch_kernel(row_count, column_count, tiles, *refs),
        in_specs=[there] * 7,
        out_specs=pl.BlockSpec(memory_space=pltpu.VMEM),
        out_shape=jax.ShapeDtypeStruct((chunks, examples, LANES), jnp.float32),
        scratch_shapes=[
            pltpu.VMEM((examples, depth, row_count), jnp.bfloat16),
            pltpu.VMEM((examples, row_count, depth), jnp.bfloat16),
            pltpu.VMEM((tiles, examples, depth, TILE), jnp.bfloat16),
            pltpu.VMEM((tiles, row_count, TILE), jnp.int32),
            pltpu.VMEM((chunks, LANES), jnp.int32),
            pltpu.VMEM((chunks, LANES), jnp.int32),
            pltpu.VMEM(row_table.shape, jnp.bfloat16),
            pltpu.VMEM(lane_table.shape, jnp.bfloat16),
            pltpu.VMEM((row_count, TILE), jnp.float32),
            pltpu.VMEM((row_blocks, 2, 2 * LANES, TILE), jnp.bfloat16),
            pltpu.VMEM((row_blocks * (column_count // LANES) * BLOCK_STRIDE, LANES), jnp.float32),
            pltpu.VMEM((chunks, LANES), jnp.float32),
            pltpu.VMEM((chunks // GROUP, GROUP, LANES), jnp.int32),
            [pltpu.SMEM((GROUP, LANES), jnp.int32)] * SLOTS,
            [pltpu.VMEM((GROUP, 2 * LANES, LANES), jnp.float32)] * 2,
            pltpu.SemaphoreType.DMA((examples, X_PIECES)),
            pltpu.SemaphoreType.DMA((tiles,)),
            pltpu.SemaphoreType.DMA((tiles,)),
            pltpu.SemaphoreType.DMA((4,)),
            pltpu.SemaphoreType.DMA((SLOTS,)),
        ],
        compiler_params=pltpu.CompilerParams(vmem_limit_bytes=60 * 1024 * 1024),
    )(inputs, up_cotangent, signs, kept_row.reshape(chunks, LANES), kept_col.reshape(chunks, LANES),
      row_table, lane_table)


def local(inputs, up_cotangent, signs, kept_row, kept_col):
    examples = inputs.shape[0]
    partial = partial_features(inputs, up_cotangent, signs, kept_row, kept_col)
    devices = lax.axis_size("grp") * lax.axis_size("shard")
    own = kept_row.shape[0] // devices
    if own % LANES:
        shares = partial.transpose(1, 0, 2).reshape(examples, devices, own).transpose(1, 0, 2)
        shares = lax.all_to_all(shares, ("grp", "shard"), 0, 0, tiled=True)
        return jnp.sum(shares, axis=0)
    shares = partial.reshape(devices, own // LANES, examples, LANES)
    shares = jnp.sum(lax.all_to_all(shares, ("grp", "shard"), 0, 0, tiled=True), axis=0)
    return shares.transpose(1, 0, 2).reshape(examples, own)


def solution(mesh):
    placed = (P(None, None, "grp"), P(None, None, "shard"), P("grp", "shard"), P(), P())
    return jax.shard_map(
        local, mesh=mesh, in_specs=placed, out_specs=P(None, ("grp", "shard")), check_vma=False
    )
```

```python
import math

import jax
import jax.numpy as jnp
import numpy as np
from jax import lax
from jax.experimental import pallas as pl
from jax.experimental.pallas import tpu as pltpu
from jax.sharding import PartitionSpec as P

D = 4096
FPAD = 16384
LANES = 128
TILE = 256
WIDE = 2
SPREAD = 256
BLOCK_STRIDE = TILE + 8
X_PIECES = 2
GROUP = 4
SLOTS = 4


def hadamard(length):
    table = np.ones((1, 1), np.float32)
    while table.shape[0] < length:
        table = np.block([[table, table], [table, -table]])
    return table


def butterflies(blocks):
    blocks = list(blocks)
    width = 1
    while width < len(blocks):
        for low in range(len(blocks)):
            if low & width:
                continue
            a, b = blocks[low], blocks[low | width]
            if b is None:
                blocks[low | width] = a
            else:
                blocks[low], blocks[low | width] = a + b, a - b
        width *= 2
    return blocks


def split(values):
    high = values.astype(jnp.bfloat16)
    low = (values - high.astype(jnp.float32)).astype(jnp.bfloat16)
    return high, low


def parity_sign(bits):
    for shift in (16, 8, 4, 2, 1):
        bits = jnp.bitwise_xor(bits, jnp.right_shift(bits, shift))
    return (1 - 2 * jnp.bitwise_and(bits, 1)).astype(jnp.float32)


def sketch_kernel(row_count, column_count, tiles,
                  x_ref, u_ref, signs_ref, kept_row_ref, kept_col_ref, twice_ref,
                  out_ref,
                  x, xt, u, signs, kept_row, kept_col, twice,
                  halves, table, factor, spot_vmem, spot_smem, stages,
                  x_sem, u_sem, signs_sem, small_sem, spot_sem):
    row_blocks = row_count // LANES
    column_blocks = column_count // LANES
    pairs = column_blocks // 2
    chunks = kept_row.shape[0]
    groups = chunks // GROUP
    group_at, shard_at = lax.axis_index("grp"), lax.axis_index("shard")
    f32 = jnp.float32

    def x_copy(e, piece):
        rows = pl.ds(piece * (x.shape[1] // X_PIECES), x.shape[1] // X_PIECES)
        return pltpu.make_async_copy(x_ref.at[e, rows], x.at[e, rows], x_sem.at[e, piece])

    first_wide = WIDE if tiles % WIDE == 0 else tiles % WIDE
    units = u.shape[0]

    def first_tile(unit):
        return first_wide + WIDE * (unit - 1)

    def u_copy(unit, tile, wide):
        source = pl.ds(pl.multiple_of(tile * TILE, TILE), wide * TILE)
        return pltpu.make_async_copy(
            u_ref.at[:, :, source], u.at[unit, :, :, pl.ds(0, wide * TILE)], u_sem.at[unit])

    def signs_copy(unit, tile, wide):
        source = pl.ds(pl.multiple_of(tile * TILE, TILE), wide * TILE)
        return pltpu.make_async_copy(
            signs_ref.at[:, source], signs.at[unit, :, pl.ds(0, wide * TILE)], signs_sem.at[unit])

    def spot_copy(at, slot):
        return pltpu.make_async_copy(spot_vmem.at[at], spot_smem[slot], spot_sem.at[slot])

    small = [pltpu.make_async_copy(source, target, small_sem.at[at]) for at, (source, target) in enumerate(
        [(kept_row_ref, kept_row), (kept_col_ref, kept_col), (twice_ref, twice)])]

    def ahead(unit):
        u_copy(unit, first_tile(unit), WIDE).start()
        signs_copy(unit, first_tile(unit), WIDE).start()

    for e in range(2):
        for piece in range(X_PIECES):
            x_copy(e, piece).start()
        if e == 0:
            u_copy(0, 0, first_wide).start()
            signs_copy(0, 0, first_wide).start()
    for copy in small:
        copy.start()

    def place(block, column_block):
        return (block * column_blocks + column_block) * BLOCK_STRIDE

    def turn(e):
        for piece in range(X_PIECES):
            x_copy(e, piece).wait()
        for block in range(row_blocks):
            cut = slice(block * LANES, (block + 1) * LANES)
            xt[e, cut, :] = x[e, :, cut].T

    def spread(e, unit, values):
        for left in range(0, values.shape[1], SPREAD):
            lanes = slice(left, left + SPREAD)
            for start in range(0, LANES, 16):
                blocks = []
                for block in range(row_blocks):
                    rows = slice(block * LANES + start, block * LANES + start + 16)
                    blocks.append(values[rows, lanes] * signs[unit, rows, lanes].astype(f32))
                for block, mixed in enumerate(butterflies(blocks)):
                    high, low = split(mixed)
                    halves[e][block, start:start + 16, lanes] = high
                    halves[e][block, LANES + start:LANES + start + 16, lanes] = low

    def gradient(e, unit, wide):
        return jnp.dot(xt[e], u[unit, e, :, :wide * TILE], preferred_element_type=f32)

    def rows_to_table(e, tile, wide):
        for block in range(row_blocks):
            whole = jnp.dot(twice[...], halves[e][block, :, :wide * TILE], preferred_element_type=f32)
            for at in range(wide):
                left = whole[:, at * TILE:at * TILE + LANES]
                right = whole[:, at * TILE + LANES:(at + 1) * TILE]
                for half, values in enumerate((left + right, left - right)):
                    base = pl.multiple_of(place(block, 2 * (tile + at) + half), 8)
                    table[pl.ds(base + e, LANES, stride=2), :] = values

    turn(0)
    u_copy(0, 0, first_wide).wait()
    first = gradient(0, 0, first_wide)
    signs_copy(0, 0, first_wide).wait()
    for copy in small:
        copy.wait()
    for unit in range(1, min(3, units)):
        ahead(unit)
    spread(0, 0, first)
    turn(1)
    second = gradient(1, 0, first_wide)
    rows_to_table(0, 0, first_wide)
    spread(1, 0, second)
    rows_to_table(1, 0, first_wide)

    row = jnp.bitwise_and(kept_row[...], row_count - 1)
    col = jnp.bitwise_and(kept_col[...], column_count - 1)
    spots = place(row // LANES, col // LANES) + jnp.bitwise_and(row, LANES - 1) * 2
    for at in range(groups):
        spot_vmem[at] = spots[at * GROUP:(at + 1) * GROUP]
    for at in range(SLOTS):
        spot_copy(at, at).start()
    factor[...] = (1.0 / math.sqrt(D * FPAD)) * parity_sign(jnp.bitwise_xor(
        jnp.bitwise_and(kept_row[...] // row_count, group_at),
        jnp.bitwise_and(kept_col[...] // column_count, shard_at)))

    def later_unit(unit, carry):
        @pl.when(unit + 2 < units)
        def _():
            ahead(unit + 2)

        tile = first_tile(unit)
        u_copy(unit, tile, WIDE).wait()
        signs_copy(unit, tile, WIDE).wait()
        first = gradient(0, unit, WIDE)
        spread(0, unit, first)
        second = gradient(1, unit, WIDE)
        rows_to_table(0, tile, WIDE)
        spread(1, unit, second)
        rows_to_table(1, tile, WIDE)
        return carry

    lax.fori_loop(1, units, later_unit, 0)

    if pairs > 1:
        part = 32

        def columns(at, carry):
            block = at // (TILE // part)
            row = (at % (TILE // part)) * part
            base = pl.multiple_of(place(block, 0) + row, 8)
            for half in range(2):
                for extra in range(0, part, 8):
                    def rows_of(pair):
                        return pl.ds(base + (2 * pair + half) * BLOCK_STRIDE + extra, 8)

                    blocks = butterflies(
                        [table[rows_of(pair), :] if pair < tiles else None for pair in range(pairs)])
                    for pair in range(pairs):
                        table[rows_of(pair), :] = blocks[pair]
            return carry

        lax.fori_loop(0, row_blocks * (TILE // part), columns, 0)

    def gather(slot, stage):
        for part in range(GROUP):
            for u_at in range(LANES):
                at = pl.multiple_of(spot_smem[slot][part, u_at], 2)
                stage[part, 2 * u_at:2 * u_at + 2, :] = table[pl.ds(at, 2), :]

    def finish(at, stage):
        for part in range(GROUP):
            finish_chunk(at * GROUP + part, stage.at[part])

    def finish_chunk(chunk, stage):
        rows = jnp.concatenate([stage[pl.ds(0, LANES, stride=2), :], stage[pl.ds(1, LANES, stride=2), :]], axis=0)
        high, low = split(rows)
        both = jnp.concatenate([high, low], axis=1)
        whole = lax.dot_general(twice[...], both, (((1,), (1,)), ((), ())), preferred_element_type=f32)
        lane = jnp.bitwise_and(kept_col[pl.ds(chunk, 1), :], LANES - 1)
        sign = factor[pl.ds(chunk, 1), :]
        mask = lax.broadcasted_iota(jnp.int32, (LANES, LANES), 0) == lane
        for e in range(2):
            picked = jnp.where(mask, whole[:, e * LANES:(e + 1) * LANES], 0.0)
            out_ref[chunk, pl.ds(e, 1), :] = jnp.sum(picked, axis=0, keepdims=True) * sign

    spot_copy(0, 0).wait()
    gather(0, stages[0])
    spot_copy(min(SLOTS, groups - 1), 0).start()

    def slots_round(turn_at, carry):
        for step in range(1, SLOTS + 1):
            at = turn_at * SLOTS + step
            slot = step % SLOTS
            spot_copy(jnp.minimum(at, groups - 1), slot).wait()
            gather(slot, stages[step % 2])
            finish(at - 1, stages[(step - 1) % 2])
            spot_copy(jnp.minimum(at + SLOTS, groups - 1), slot).start()
        return carry

    lax.fori_loop(0, groups // SLOTS, slots_round, 0)
    for slot in range(SLOTS):
        spot_copy(groups - 1, slot).wait()


def partial_features(inputs, up_cotangent, signs, kept_row, kept_col):
    examples, depth, row_count = inputs.shape
    column_count = signs.shape[1]
    if up_cotangent.shape[2] % TILE:
        extra = -up_cotangent.shape[2] % TILE
        up_cotangent = jnp.pad(up_cotangent, ((0, 0), (0, 0), (0, extra)))
    tiles = up_cotangent.shape[2] // TILE
    chunks = kept_row.shape[0] // LANES
    twice = jnp.asarray(np.concatenate([hadamard(LANES)] * 2, axis=1), jnp.bfloat16)
    there = pl.BlockSpec(memory_space=pl.ANY)
    row_blocks = row_count // LANES
    units = -(-tiles // WIDE)
    return pl.pallas_call(
        lambda *refs: sketch_kernel(row_count, column_count, tiles, *refs),
        in_specs=[there] * 6,
        out_specs=pl.BlockSpec(memory_space=pltpu.VMEM),
        out_shape=jax.ShapeDtypeStruct((chunks, examples, LANES), jnp.float32),
        scratch_shapes=[
            pltpu.VMEM((examples, depth, row_count), jnp.bfloat16),
            pltpu.VMEM((examples, row_count, depth), jnp.bfloat16),
            pltpu.VMEM((units, examples, depth, WIDE * TILE), jnp.bfloat16),
            pltpu.VMEM((units, row_count, WIDE * TILE), jnp.int32),
            pltpu.VMEM((chunks, LANES), jnp.int32),
            pltpu.VMEM((chunks, LANES), jnp.int32),
            pltpu.VMEM(twice.shape, jnp.bfloat16),
            [pltpu.VMEM((row_blocks, 2 * LANES, WIDE * TILE), jnp.bfloat16)] * 2,
            pltpu.VMEM((row_blocks * (column_count // LANES) * BLOCK_STRIDE, LANES), jnp.float32),
            pltpu.VMEM((chunks, LANES), jnp.float32),
            pltpu.VMEM((chunks // GROUP, GROUP, LANES), jnp.int32),
            [pltpu.SMEM((GROUP, LANES), jnp.int32)] * SLOTS,
            [pltpu.VMEM((GROUP, 2 * LANES, LANES), jnp.float32)] * 2,
            pltpu.SemaphoreType.DMA((examples, X_PIECES)),
            pltpu.SemaphoreType.DMA((units,)),
            pltpu.SemaphoreType.DMA((units,)),
            pltpu.SemaphoreType.DMA((3,)),
            pltpu.SemaphoreType.DMA((SLOTS,)),
        ],
        compiler_params=pltpu.CompilerParams(vmem_limit_bytes=60 * 1024 * 1024),
    )(inputs, up_cotangent, signs, kept_row.reshape(chunks, LANES), kept_col.reshape(chunks, LANES),
      twice)


def local(inputs, up_cotangent, signs, kept_row, kept_col):
    examples = inputs.shape[0]
    partial = partial_features(inputs, up_cotangent, signs, kept_row, kept_col)
    devices = lax.axis_size("grp") * lax.axis_size("shard")
    own = kept_row.shape[0] // devices
    if own % LANES:
        shares = partial.transpose(1, 0, 2).reshape(examples, devices, own).transpose(1, 0, 2)
        shares = lax.all_to_all(shares, ("grp", "shard"), 0, 0, tiled=True)
        return jnp.sum(shares, axis=0)
    shares = partial.reshape(devices, own // LANES, examples, LANES)
    shares = jnp.sum(lax.all_to_all(shares, ("grp", "shard"), 0, 0, tiled=True), axis=0)
    return shares.transpose(1, 0, 2).reshape(examples, own)


def solution(mesh):
    placed = (P(None, None, "grp"), P(None, None, "shard"), P("grp", "shard"), P(), P())
    return jax.shard_map(
        local, mesh=mesh, in_specs=placed, out_specs=P(None, ("grp", "shard")), check_vma=False
    )
```

```python
import math

import jax
import jax.numpy as jnp
import numpy as np
from jax import lax
from jax.experimental import pallas as pl
from jax.experimental.pallas import tpu as pltpu
from jax.sharding import PartitionSpec as P

D = 4096
FPAD = 16384
LANES = 128
TILE = 256
WIDE = 2
SPREAD = 256
BLOCK_STRIDE = TILE + 8
X_PIECES = 2
PART = 128
STAGES = 8


def hadamard(length):
    table = np.ones((1, 1), np.float32)
    while table.shape[0] < length:
        table = np.block([[table, table], [table, -table]])
    return table


def butterflies(blocks):
    blocks = list(blocks)
    width = 1
    while width < len(blocks):
        for low in range(len(blocks)):
            if low & width:
                continue
            a, b = blocks[low], blocks[low | width]
            if b is None:
                blocks[low | width] = a
            else:
                blocks[low], blocks[low | width] = a + b, a - b
        width *= 2
    return blocks


def split(values):
    high = values.astype(jnp.bfloat16)
    low = (values - high.astype(jnp.float32)).astype(jnp.bfloat16)
    return high, low


def parity_sign(bits):
    for shift in (16, 8, 4, 2, 1):
        bits = jnp.bitwise_xor(bits, jnp.right_shift(bits, shift))
    return (1 - 2 * jnp.bitwise_and(bits, 1)).astype(jnp.float32)


def sketch_kernel(row_count, column_count, tiles,
                  x_ref, u_ref, signs_ref, kept_row_ref, kept_col_ref, twice_ref,
                  out_ref,
                  x, xt, u, signs, kept_row, kept_col, twice,
                  halves, table, factor, spot_vmem, spot_smem, stages,
                  x_sem, u_sem, signs_sem, small_sem, spot_sem):
    row_blocks = row_count // LANES
    column_blocks = column_count // LANES
    chunks = kept_row.shape[0]
    group_at, shard_at = lax.axis_index("grp"), lax.axis_index("shard")
    f32 = jnp.float32

    def x_copy(e, piece):
        rows = pl.ds(piece * (x.shape[1] // X_PIECES), x.shape[1] // X_PIECES)
        return pltpu.make_async_copy(x_ref.at[e, rows], x.at[e, rows], x_sem.at[e, piece])

    first_wide = WIDE if tiles % WIDE == 0 else tiles % WIDE
    last = tiles - first_wide
    units = u.shape[0]

    def first_tile(unit):
        return WIDE * (unit - 1)

    def u_copy(unit, tile, wide):
        source = pl.ds(pl.multiple_of(tile * TILE, TILE), wide * TILE)
        return pltpu.make_async_copy(
            u_ref.at[:, :, source], u.at[unit, :, :, pl.ds(0, wide * TILE)], u_sem.at[unit])

    def signs_copy(unit, tile, wide):
        source = pl.ds(pl.multiple_of(tile * TILE, TILE), wide * TILE)
        return pltpu.make_async_copy(
            signs_ref.at[:, source], signs.at[unit, :, pl.ds(0, wide * TILE)], signs_sem.at[unit])

    spot_copy = pltpu.make_async_copy(spot_vmem, spot_smem, spot_sem)

    small = [pltpu.make_async_copy(source, target, small_sem.at[at]) for at, (source, target) in enumerate(
        [(kept_row_ref, kept_row), (kept_col_ref, kept_col), (twice_ref, twice)])]

    def ahead(unit):
        u_copy(unit, first_tile(unit), WIDE).start()
        signs_copy(unit, first_tile(unit), WIDE).start()

    for e in range(2):
        for piece in range(X_PIECES):
            x_copy(e, piece).start()
        if e == 0:
            u_copy(0, last, first_wide).start()
            signs_copy(0, last, first_wide).start()
    for copy in small:
        copy.start()

    def place(block, column_block):
        return (block * column_blocks + column_block) * BLOCK_STRIDE

    def turn(e):
        for piece in range(X_PIECES):
            x_copy(e, piece).wait()
        for block in range(row_blocks):
            cut = slice(block * LANES, (block + 1) * LANES)
            xt[e, cut, :] = x[e, :, cut].T

    def spread(e, unit, values):
        for left in range(0, values.shape[1], SPREAD):
            lanes = slice(left, left + SPREAD)
            for start in range(0, LANES, 16):
                blocks = []
                for block in range(row_blocks):
                    rows = slice(block * LANES + start, block * LANES + start + 16)
                    blocks.append(values[rows, lanes] * signs[unit, rows, lanes].astype(f32))
                for block, mixed in enumerate(butterflies(blocks)):
                    high, low = split(mixed)
                    halves[e][block, start:start + 16, lanes] = high
                    halves[e][block, LANES + start:LANES + start + 16, lanes] = low

    def gradient(e, unit, wide):
        return jnp.dot(xt[e], u[unit, e, :, :wide * TILE], preferred_element_type=f32)

    def rows_to_table(e, tile, wide):
        for block in range(row_blocks):
            whole = jnp.dot(twice[...], halves[e][block, :, :wide * TILE], preferred_element_type=f32)
            parts = butterflies([whole[:, at:at + LANES] for at in range(0, wide * TILE, LANES)])
            for at, values in enumerate(parts):
                base = pl.multiple_of(place(block, 2 * tile + at), 8)
                table[pl.ds(base + e, LANES, stride=2), :] = values

    turn(0)
    u_copy(0, last, first_wide).wait()
    first = gradient(0, 0, first_wide)
    signs_copy(0, last, first_wide).wait()
    for copy in small:
        copy.wait()
    for unit in range(1, min(3, units)):
        ahead(unit)
    spread(0, 0, first)
    turn(1)
    second = gradient(1, 0, first_wide)
    rows_to_table(0, last, first_wide)
    spread(1, 0, second)
    rows_to_table(1, last, first_wide)

    row = jnp.bitwise_and(kept_row[...], row_count - 1)
    col = jnp.bitwise_and(kept_col[...], column_count - 1)
    spot_vmem[...] = place(row // LANES, col // LANES) + jnp.bitwise_and(row, LANES - 1) * 2
    spot_copy.start()
    factor[...] = (1.0 / math.sqrt(D * FPAD)) * parity_sign(jnp.bitwise_xor(
        jnp.bitwise_and(kept_row[...] // row_count, group_at),
        jnp.bitwise_and(kept_col[...] // column_count, shard_at)))

    def later_unit(unit, carry):
        @pl.when(unit + 2 < units)
        def _():
            ahead(unit + 2)

        tile = first_tile(unit)
        u_copy(unit, tile, WIDE).wait()
        signs_copy(unit, tile, WIDE).wait()
        first = gradient(0, unit, WIDE)
        spread(0, unit, first)
        second = gradient(1, unit, WIDE)
        rows_to_table(0, tile, WIDE)
        spread(1, unit, second)
        rows_to_table(1, tile, WIDE)
        return carry

    lax.fori_loop(1, units, later_unit, 0)

    quads = column_blocks // (2 * WIDE)
    if quads > 1:
        def columns(at, carry):
            block = at // (TILE // PART)
            row = (at % (TILE // PART)) * PART
            base = pl.multiple_of(place(block, 0) + row, 8)
            for extra in range(0, PART, 8):
                def rows_of(quad, inner):
                    return pl.ds(base + (2 * WIDE * quad + inner) * BLOCK_STRIDE + extra, 8)

                loaded = {}
                for inner in range(2 * WIDE):
                    blocks = []
                    for quad in range(quads):
                        present = min(max(tiles - WIDE * quad, 0), WIDE) * 2
                        if present:
                            key = quad, inner % present
                            if key not in loaded:
                                loaded[key] = table[rows_of(*key), :]
                        blocks.append(loaded[key] if present else None)
                    blocks = butterflies(blocks)
                    for quad in range(quads):
                        table[rows_of(quad, inner), :] = blocks[quad]
            return carry

        lax.fori_loop(0, row_blocks * (TILE // PART), columns, 0)

    def gather(chunk, stage):
        for u_at in range(LANES):
            at = pl.multiple_of(spot_smem[chunk, u_at], 2)
            stage[2 * u_at:2 * u_at + 2, :] = table[pl.ds(at, 2), :]

    def finish_chunk(chunk, stage):
        col = jnp.broadcast_to(kept_col[pl.ds(chunk, 1), :], (8, LANES))
        flips = [(1 - 2 * jnp.bitwise_and(jnp.right_shift(col, bit), 1)).astype(f32) for bit in range(3, 7)]
        bits = jnp.bitwise_and(col, lax.broadcasted_iota(jnp.int32, (8, LANES), 0))
        bits = jnp.bitwise_xor(bits, jnp.bitwise_xor(jnp.right_shift(bits, 1), jnp.right_shift(bits, 2)))
        weights = (1 - 2 * jnp.bitwise_and(bits, 1)).astype(f32) * factor[pl.ds(chunk, 1), :]
        for e in range(2):
            turned = stage[pl.ds(e, LANES, stride=2), :].T
            parts = [turned[start:start + 8] for start in range(0, LANES, 8)]
            for flip in flips:
                parts = [low + high * flip for low, high in zip(parts[0::2], parts[1::2])]
            out_ref[chunk, pl.ds(e, 1), :] = jnp.sum(parts[0] * weights, axis=0, keepdims=True)

    spot_copy.wait()
    for chunk in range(chunks):
        gather(chunk, stages[chunk % len(stages)])
        finish_chunk(chunk, stages[chunk % len(stages)])


def partial_features(inputs, up_cotangent, signs, kept_row, kept_col):
    examples, depth, row_count = inputs.shape
    column_count = signs.shape[1]
    if up_cotangent.shape[2] % TILE:
        extra = -up_cotangent.shape[2] % TILE
        up_cotangent = jnp.pad(up_cotangent, ((0, 0), (0, 0), (0, extra)))
    tiles = up_cotangent.shape[2] // TILE
    chunks = kept_row.shape[0] // LANES
    twice = jnp.asarray(np.concatenate([hadamard(LANES)] * 2, axis=1), jnp.bfloat16)
    there = pl.BlockSpec(memory_space=pl.ANY)
    row_blocks = row_count // LANES
    units = -(-tiles // WIDE)
    return pl.pallas_call(
        lambda *refs: sketch_kernel(row_count, column_count, tiles, *refs),
        in_specs=[there] * 6,
        out_specs=pl.BlockSpec(memory_space=pltpu.VMEM),
        out_shape=jax.ShapeDtypeStruct((chunks, examples, LANES), jnp.float32),
        scratch_shapes=[
            pltpu.VMEM((examples, depth, row_count), jnp.bfloat16),
            pltpu.VMEM((examples, row_count, depth), jnp.bfloat16),
            pltpu.VMEM((units, examples, depth, WIDE * TILE), jnp.bfloat16),
            pltpu.VMEM((units, row_count, WIDE * TILE), jnp.int32),
            pltpu.VMEM((chunks, LANES), jnp.int32),
            pltpu.VMEM((chunks, LANES), jnp.int32),
            pltpu.VMEM(twice.shape, jnp.bfloat16),
            [pltpu.VMEM((row_blocks, 2 * LANES, WIDE * TILE), jnp.bfloat16)] * 2,
            pltpu.VMEM((row_blocks * (column_count // LANES) * BLOCK_STRIDE, LANES), jnp.float32),
            pltpu.VMEM((chunks, LANES), jnp.float32),
            pltpu.VMEM((chunks, LANES), jnp.int32),
            pltpu.SMEM((chunks, LANES), jnp.int32),
            [pltpu.VMEM((2 * LANES, LANES), jnp.float32)] * STAGES,
            pltpu.SemaphoreType.DMA((examples, X_PIECES)),
            pltpu.SemaphoreType.DMA((units,)),
            pltpu.SemaphoreType.DMA((units,)),
            pltpu.SemaphoreType.DMA((3,)),
            pltpu.SemaphoreType.DMA,
        ],
        compiler_params=pltpu.CompilerParams(vmem_limit_bytes=60 * 1024 * 1024),
    )(inputs, up_cotangent, signs, kept_row.reshape(chunks, LANES), kept_col.reshape(chunks, LANES),
      twice)


def local(inputs, up_cotangent, signs, kept_row, kept_col):
    examples = inputs.shape[0]
    partial = partial_features(inputs, up_cotangent, signs, kept_row, kept_col)
    devices = lax.axis_size("grp") * lax.axis_size("shard")
    own = kept_row.shape[0] // devices
    if own % LANES:
        shares = partial.transpose(1, 0, 2).reshape(examples, devices, own).transpose(1, 0, 2)
        shares = lax.all_to_all(shares, ("grp", "shard"), 0, 0, tiled=True)
        return jnp.sum(shares, axis=0)
    shares = partial.reshape(devices, own // LANES, examples, LANES)
    shares = jnp.sum(lax.all_to_all(shares, ("grp", "shard"), 0, 0, tiled=True), axis=0)
    return shares.transpose(1, 0, 2).reshape(examples, own)


def solution(mesh):
    placed = (P(None, None, "grp"), P(None, None, "shard"), P("grp", "shard"), P(), P())
    return jax.shard_map(
        local, mesh=mesh, in_specs=placed, out_specs=P(None, ("grp", "shard")), check_vma=False
    )
```

```python
import math

import jax
import jax.numpy as jnp
import numpy as np
from jax import lax
from jax.experimental import pallas as pl
from jax.experimental.pallas import tpu as pltpu
from jax.sharding import PartitionSpec as P

D = 4096
FPAD = 16384
LANES = 128
TILE = 256
WIDE = 2
SPREAD = 256
BLOCK_STRIDE = TILE + 8
X_PIECES = 4
PART = 128
STAGES = 8


def hadamard(length):
    table = np.ones((1, 1), np.float32)
    while table.shape[0] < length:
        table = np.block([[table, table], [table, -table]])
    return table


def butterflies(blocks):
    blocks = list(blocks)
    width = 1
    while width < len(blocks):
        for low in range(len(blocks)):
            if low & width:
                continue
            a, b = blocks[low], blocks[low | width]
            if b is None:
                blocks[low | width] = a
            else:
                blocks[low], blocks[low | width] = a + b, a - b
        width *= 2
    return blocks


def split(values):
    high = values.astype(jnp.bfloat16)
    low = (values - high.astype(jnp.float32)).astype(jnp.bfloat16)
    return high, low


def parity_sign(bits):
    for shift in (16, 8, 4, 2, 1):
        bits = jnp.bitwise_xor(bits, jnp.right_shift(bits, shift))
    return (1 - 2 * jnp.bitwise_and(bits, 1)).astype(jnp.float32)


def sketch_kernel(row_count, column_count, tiles,
                  x_ref, u_ref, signs_ref, kept_row_ref, kept_col_ref, twice_ref,
                  out_ref,
                  x, xt, u, signs, kept_row, kept_col, twice,
                  halves, table, factor, spot_vmem, spot_smem, stages,
                  x_sem, u_sem, signs_sem, small_sem, spot_sem):
    row_blocks = row_count // LANES
    column_blocks = column_count // LANES
    chunks = kept_row.shape[0]
    group_at, shard_at = lax.axis_index("grp"), lax.axis_index("shard")
    f32 = jnp.float32

    def x_copy(e, piece):
        rows = pl.ds(piece * (x.shape[1] // X_PIECES), x.shape[1] // X_PIECES)
        return pltpu.make_async_copy(x_ref.at[e, rows], x.at[e, rows], x_sem.at[e, piece])

    first_wide = WIDE if tiles % WIDE == 0 else tiles % WIDE
    last = tiles - first_wide
    units = u.shape[0]

    def first_tile(unit):
        return WIDE * (unit - 1)

    def u_copy(unit, tile, wide):
        source = pl.ds(pl.multiple_of(tile * TILE, TILE), wide * TILE)
        return pltpu.make_async_copy(
            u_ref.at[:, :, source], u.at[unit, :, :, pl.ds(0, wide * TILE)], u_sem.at[unit])

    def signs_copy(unit, tile, wide):
        source = pl.ds(pl.multiple_of(tile * TILE, TILE), wide * TILE)
        return pltpu.make_async_copy(
            signs_ref.at[:, source], signs.at[unit, :, pl.ds(0, wide * TILE)], signs_sem.at[unit])

    spot_copy = pltpu.make_async_copy(spot_vmem, spot_smem, spot_sem)

    small = [pltpu.make_async_copy(source, target, small_sem.at[at]) for at, (source, target) in enumerate(
        [(kept_row_ref, kept_row), (kept_col_ref, kept_col), (twice_ref, twice)])]

    def ahead(unit):
        u_copy(unit, first_tile(unit), WIDE).start()
        signs_copy(unit, first_tile(unit), WIDE).start()

    for e in range(2):
        for piece in range(X_PIECES):
            x_copy(e, piece).start()
        if e == 0:
            u_copy(0, last, first_wide).start()
            signs_copy(0, last, first_wide).start()
    for copy in small:
        copy.start()

    def place(block, column_block):
        return (block * column_blocks + column_block) * BLOCK_STRIDE

    def turn(e):
        for block in range(row_blocks):
            cut = slice(block * LANES, (block + 1) * LANES)
            xt[e, cut, :] = x[e, :, cut].T

    def spread(unit, both):
        for left in range(0, both[0].shape[1], SPREAD):
            lanes = slice(left, left + SPREAD)
            for start in range(0, LANES, 16):
                places = [slice(block * LANES + start, block * LANES + start + 16) for block in range(row_blocks)]
                coins = [signs[unit, rows, lanes].astype(f32) for rows in places]
                for e in range(2):
                    blocks = butterflies([both[e][rows, lanes] * coin for rows, coin in zip(places, coins)])
                    for block, mixed in enumerate(blocks):
                        high, low = split(mixed)
                        halves[e][block, start:start + 16, lanes] = high
                        halves[e][block, LANES + start:LANES + start + 16, lanes] = low

    def gradient(e, unit, wide):
        return jnp.dot(xt[e], u[unit, e, :, :wide * TILE], preferred_element_type=f32)

    def rows_to_table(e, tile, wide):
        for block in range(row_blocks):
            whole = jnp.dot(twice[...], halves[e][block, :, :wide * TILE], preferred_element_type=f32)
            parts = butterflies([whole[:, at:at + LANES] for at in range(0, wide * TILE, LANES)])
            for at, values in enumerate(parts):
                base = pl.multiple_of(place(block, 2 * tile + at), 8)
                table[pl.ds(base + e, LANES, stride=2), :] = values

    for e in range(2):
        for piece in range(X_PIECES):
            x_copy(e, piece).wait()
    u_copy(0, last, first_wide).wait()
    for copy in small:
        copy.wait()
    signs_copy(0, last, first_wide).wait()
    for unit in range(1, min(3, units)):
        ahead(unit)
    turn(0)
    first = gradient(0, 0, first_wide)
    turn(1)
    second = gradient(1, 0, first_wide)
    spread(0, (first, second))
    for e in range(2):
        rows_to_table(e, last, first_wide)

    row = jnp.bitwise_and(kept_row[...], row_count - 1)
    col = jnp.bitwise_and(kept_col[...], column_count - 1)
    spot_vmem[...] = place(row // LANES, col // LANES) + jnp.bitwise_and(row, LANES - 1) * 2
    spot_copy.start()
    factor[...] = (1.0 / math.sqrt(D * FPAD)) * parity_sign(jnp.bitwise_xor(
        jnp.bitwise_and(kept_row[...] // row_count, group_at),
        jnp.bitwise_and(kept_col[...] // column_count, shard_at)))

    def later_unit(unit, carry):
        @pl.when(unit + 2 < units)
        def _():
            ahead(unit + 2)

        tile = first_tile(unit)
        u_copy(unit, tile, WIDE).wait()
        signs_copy(unit, tile, WIDE).wait()
        first = gradient(0, unit, WIDE)
        second = gradient(1, unit, WIDE)
        spread(unit, (first, second))
        for e in range(2):
            rows_to_table(e, tile, WIDE)
        return carry

    lax.fori_loop(1, units, later_unit, 0)

    quads = column_blocks // (2 * WIDE)
    if quads > 1:
        def columns(at, carry):
            block = at // (TILE // PART)
            row = (at % (TILE // PART)) * PART
            base = pl.multiple_of(place(block, 0) + row, 8)
            for extra in range(0, PART, 8):
                def rows_of(quad, inner):
                    return pl.ds(base + (2 * WIDE * quad + inner) * BLOCK_STRIDE + extra, 8)

                loaded = {}
                for inner in range(2 * WIDE):
                    blocks = []
                    for quad in range(quads):
                        present = min(max(tiles - WIDE * quad, 0), WIDE) * 2
                        if present:
                            key = quad, inner % present
                            if key not in loaded:
                                loaded[key] = table[rows_of(*key), :]
                        blocks.append(loaded[key] if present else None)
                    blocks = butterflies(blocks)
                    for quad in range(quads):
                        table[rows_of(quad, inner), :] = blocks[quad]
            return carry

        lax.fori_loop(0, row_blocks * (TILE // PART), columns, 0)

    def gather(chunk, stage):
        for u_at in range(LANES):
            at = pl.multiple_of(spot_smem[chunk, u_at], 2)
            stage[2 * u_at:2 * u_at + 2, :] = table[pl.ds(at, 2), :]

    def finish_chunk(chunk, stage):
        col = jnp.broadcast_to(kept_col[pl.ds(chunk, 1), :], (8, LANES))
        flips = [(1 - 2 * jnp.bitwise_and(jnp.right_shift(col, bit), 1)).astype(f32) for bit in range(3, 7)]
        bits = jnp.bitwise_and(col, lax.broadcasted_iota(jnp.int32, (8, LANES), 0))
        bits = jnp.bitwise_xor(bits, jnp.bitwise_xor(jnp.right_shift(bits, 1), jnp.right_shift(bits, 2)))
        weights = (1 - 2 * jnp.bitwise_and(bits, 1)).astype(f32) * factor[pl.ds(chunk, 1), :]
        for e in range(2):
            turned = stage[pl.ds(e, LANES, stride=2), :].T
            parts = [turned[start:start + 8] for start in range(0, LANES, 8)]
            for flip in flips:
                parts = [low + high * flip for low, high in zip(parts[0::2], parts[1::2])]
            out_ref[chunk, pl.ds(e, 1), :] = jnp.sum(parts[0] * weights, axis=0, keepdims=True)

    spot_copy.wait()
    for chunk in range(chunks):
        gather(chunk, stages[chunk % len(stages)])
        finish_chunk(chunk, stages[chunk % len(stages)])


def partial_features(inputs, up_cotangent, signs, kept_row, kept_col):
    examples, depth, row_count = inputs.shape
    column_count = signs.shape[1]
    if up_cotangent.shape[2] % TILE:
        extra = -up_cotangent.shape[2] % TILE
        up_cotangent = jnp.pad(up_cotangent, ((0, 0), (0, 0), (0, extra)))
    tiles = up_cotangent.shape[2] // TILE
    chunks = kept_row.shape[0] // LANES
    twice = jnp.asarray(np.concatenate([hadamard(LANES)] * 2, axis=1), jnp.bfloat16)
    there = pl.BlockSpec(memory_space=pl.ANY)
    row_blocks = row_count // LANES
    units = -(-tiles // WIDE)
    return pl.pallas_call(
        lambda *refs: sketch_kernel(row_count, column_count, tiles, *refs),
        in_specs=[there] * 6,
        out_specs=pl.BlockSpec(memory_space=pltpu.VMEM),
        out_shape=jax.ShapeDtypeStruct((chunks, examples, LANES), jnp.float32),
        scratch_shapes=[
            pltpu.VMEM((examples, depth, row_count), jnp.bfloat16),
            pltpu.VMEM((examples, row_count, depth), jnp.bfloat16),
            pltpu.VMEM((units, examples, depth, WIDE * TILE), jnp.bfloat16),
            pltpu.VMEM((units, row_count, WIDE * TILE), jnp.int32),
            pltpu.VMEM((chunks, LANES), jnp.int32),
            pltpu.VMEM((chunks, LANES), jnp.int32),
            pltpu.VMEM(twice.shape, jnp.bfloat16),
            [pltpu.VMEM((row_blocks, 2 * LANES, WIDE * TILE), jnp.bfloat16)] * 2,
            pltpu.VMEM((row_blocks * (column_count // LANES) * BLOCK_STRIDE, LANES), jnp.float32),
            pltpu.VMEM((chunks, LANES), jnp.float32),
            pltpu.VMEM((chunks, LANES), jnp.int32),
            pltpu.SMEM((chunks, LANES), jnp.int32),
            [pltpu.VMEM((2 * LANES, LANES), jnp.float32)] * STAGES,
            pltpu.SemaphoreType.DMA((examples, X_PIECES)),
            pltpu.SemaphoreType.DMA((units,)),
            pltpu.SemaphoreType.DMA((units,)),
            pltpu.SemaphoreType.DMA((3,)),
            pltpu.SemaphoreType.DMA,
        ],
        compiler_params=pltpu.CompilerParams(vmem_limit_bytes=60 * 1024 * 1024),
    )(inputs, up_cotangent, signs, kept_row.reshape(chunks, LANES), kept_col.reshape(chunks, LANES),
      twice)


def local(inputs, up_cotangent, signs, kept_row, kept_col):
    examples = inputs.shape[0]
    partial = partial_features(inputs, up_cotangent, signs, kept_row, kept_col)
    devices = lax.axis_size("grp") * lax.axis_size("shard")
    own = kept_row.shape[0] // devices
    if own % LANES:
        shares = partial.transpose(1, 0, 2).reshape(examples, devices, own).transpose(1, 0, 2)
        shares = lax.all_to_all(shares, ("grp", "shard"), 0, 0, tiled=True)
        return jnp.sum(shares, axis=0)
    shares = partial.reshape(devices, own // LANES, examples, LANES)
    shares = jnp.sum(lax.all_to_all(shares, ("grp", "shard"), 0, 0, tiled=True), axis=0)
    return shares.transpose(1, 0, 2).reshape(examples, own)


def solution(mesh):
    placed = (P(None, None, "grp"), P(None, None, "shard"), P("grp", "shard"), P(), P())
    return jax.shard_map(
        local, mesh=mesh, in_specs=placed, out_specs=P(None, ("grp", "shard")), check_vma=False
    )
```
